32 devices in a mesh: row: 4 (over x, core), col: 8 (over z, y).
Axes of the slice: x: 2, y: 2, z: 4, core: 2. Of those that a mesh axis runs over, the one named last changes fastest.
Arguments:
- states: bfloat16 [4096, 384], P(('row', 'col')), may hold values from -6 to 6
- mix_weight: bfloat16 [384, 384], replicated, may hold values from -0.3125 to 0.3125
- coherence: bfloat16 [4, 8, 32, 128, 128], P('row', 'col'), may hold values from -0.125 to 0.125
- block_row: int32 [4, 8, 32], P('row', 'col'), may hold values from 0 to 3, as said below
- block_col: int32 [4, 8, 32], P('row', 'col'), may hold values from 0 to 3
- block_count: int32 [4, 8], P('row', 'col'), may hold values from 8 to 32, as said below
- gain: float32 [384], replicated, may hold values from 0.5 to 1.5
- bias: float32 [384], replicated, may hold values from -3 to 3
Outputs:
- linked: bfloat16 [4096, 384], P(('row', 'col'))
The draws below stay inside these ranges and needn't reach their ends.
Inputs may be any that keep to these rules, and one draw needn't show every extreme that they name: `block_count`: no device has more than 32 live slots, and some device has exactly 32. `block_row`: at most 8 of one device's slots name any one block row; in each column group some block row is named by 8 live slots of every device.
All inputs are finite; a program needn't handle non-finite values.
Results may differ from the reference program's by a relative error of at most 0.014.
Values may be sent and summed in bfloat16 or wider, within the bound.
A program may use at most 64 MiB of HBM per device.

```python
import jax
import jax.numpy as jnp
from jax import lax

H = 384
BLK = 128
MAXB = 32
ITERS = 2
CAP = 8
NC = 4096
N_ROW = 4
N_COL = 8


def draw_block_row(key, part):
    first_key, second_key, third_key = jax.random.split(jax.random.fold_in(key, 17), 3)
    chosen = jax.random.randint(first_key, (N_COL,), 0, N_ROW)
    row_iota = jnp.arange(N_ROW, dtype=jnp.int32)
    row_scores = jax.random.randint(second_key, (N_ROW, N_COL, N_ROW), 0, 1048576) * N_ROW + row_iota
    row_scores = jnp.where(row_iota[None, None, :] == chosen[None, :, None], -1, row_scores)
    row_order = jnp.argsort(row_scores, axis=-1, stable=True).astype(jnp.int32)
    seat_group = jnp.arange(MAXB, dtype=jnp.int32) // CAP
    seat_rows = jnp.take_along_axis(row_order, jnp.broadcast_to(seat_group, (N_ROW, N_COL, MAXB)), axis=-1)
    slot_iota = jnp.arange(MAXB, dtype=jnp.int32)
    slot_scores = jax.random.randint(third_key, (N_ROW, N_COL, MAXB), 0, 1048576) * MAXB + slot_iota
    slot_scores = jnp.where(slot_iota[None, None, :] < CAP, -1 - (CAP - slot_iota[None, None, :]), slot_scores)
    slot_order = jnp.argsort(slot_scores, axis=-1, stable=True).astype(jnp.int32)
    return jnp.take_along_axis(seat_rows, slot_order, axis=-1).astype(jnp.int32)


def draw_block_count(key, part):
    first_key, second_key, third_key = jax.random.split(key, 3)
    divisor = jax.random.randint(first_key, (N_ROW, N_COL), 1, 5)
    counts = jnp.maximum(MAXB // divisor, CAP).astype(jnp.int32)
    row_pick = jax.random.randint(second_key, (), 0, N_ROW)
    col_pick = jax.random.randint(third_key, (), 0, N_COL)
    return counts.at[row_pick, col_pick].set(MAXB).astype(jnp.int32)


def touch_ends(array, rng, least, high):
    dims = array.shape
    place = [jax.random.randint(jax.random.fold_in(rng, axis), (), 0, dims[axis]) for axis in range(len(dims))]
    array = array.at[tuple(place)].set(least)
    longest = dims.index(max(dims))
    place[longest] = (place[longest] + 1) % dims[longest]
    return array.at[tuple(place)].set(high)


def steps_of(key, extent, cuts, least, high):
    def one(dim, parts):
        steps = jax.random.uniform(jax.random.fold_in(jax.random.fold_in(key, 6), dim), (parts,), jnp.float32, least / len(cuts), high / len(cuts))
        return jnp.repeat(jnp.exp(steps), extent[dim] // parts).reshape((-1,) + (1,) * (len(extent) - dim - 1))

    factor_of = one(*cuts[0])
    for cut in cuts[1:]:
        factor_of = factor_of * one(*cut)
    return factor_of


def normal_values(stream_key, shape, width, most, cuts=(), kind=jnp.bfloat16):
    entries = jax.random.normal(stream_key, shape, jnp.float32) * width
    if len(cuts) > 0:
        entries = steps_of(stream_key, shape, cuts, -0.22, 0.18) * entries
    return jnp.clip(entries, min=-most, max=most).astype(kind)


def setup_inputs(seed: int = 0) -> dict:
    seeds = jax.random.split(jax.random.key(seed), 9)
    return {
        "states": normal_values(seeds[0], (NC, H), 1.0, 6.0, ((0, 32),)),
        "mix_weight": normal_values(seeds[1], (H, H), H ** -0.5, 0.3125),
        "coherence": normal_values(seeds[2], (N_ROW, N_COL, MAXB, BLK, BLK), (MAXB * BLK // 2) ** -0.5, 0.125, ((0, 4), (1, 8))),
        "block_row": draw_block_row(jax.random.fold_in(seeds[8], 71), 0),
        "block_col": touch_ends(jax.random.randint(seeds[4], (N_ROW, N_COL, MAXB), 0, N_ROW), jax.random.fold_in(seeds[4], 1), 0, N_ROW - 1).astype(jnp.int32),
        "block_count": draw_block_count(jax.random.fold_in(seeds[8], 71), 0),
        "gain": jnp.clip(1.0 + 0.1 * jax.random.normal(seeds[6], (H,), jnp.float32), 0.5, 1.5),
        "bias": normal_values(seeds[7], (H,), 0.5, 3.0, (), jnp.float32),
    }


def normalize(hidden, coupled, gain, bias):
    summed_in = hidden.astype(jnp.float32) + coupled
    mean_value = lax.optimization_barrier(jnp.mean(summed_in, axis=-1, keepdims=True))
    centered = summed_in - mean_value
    variance = lax.optimization_barrier(jnp.mean(centered * centered, axis=-1, keepdims=True))
    return (centered * lax.rsqrt(variance + 1e-05) * gain + bias).astype(jnp.bfloat16)

def reference(states, mix_weight, coherence, block_row, block_col, block_count, gain, bias):
    slice_rows = BLK // N_COL
    grid_states = states.reshape(N_ROW, N_COL, N_COL, slice_rows, H)
    grid_states = jnp.transpose(grid_states, (2, 0, 1, 3, 4)).reshape(N_COL, N_ROW, BLK, H)
    slot_ids = jnp.arange(MAXB, dtype=jnp.int32)
    targets = jnp.arange(N_ROW, dtype=jnp.int32)
    blocks_t = jnp.transpose(coherence, (1, 0, 2, 3, 4))
    rows_t = jnp.transpose(block_row, (1, 0, 2))
    cols_t = jnp.transpose(block_col, (1, 0, 2))
    counts_t = jnp.transpose(block_count, (1, 0))

    def couple_group(group_args):
        mixed, blocks, row_ids, col_ids, counts = group_args
        pieces = mixed[col_ids].astype(jnp.float32)
        products_f = jnp.einsum('rkab,rkbh->rkah', blocks.astype(jnp.float32), pieces, precision=lax.Precision.HIGHEST)
        live_mask = slot_ids[None, :] < counts[:, None]
        onehot = ((row_ids[:, None, :] == targets[None, :, None]) & live_mask[:, None, :]).astype(jnp.float32)
        terms = jnp.einsum('rik,rkah->riah', onehot, products_f, precision=lax.Precision.HIGHEST).astype(jnp.bfloat16)
        return lax.optimization_barrier(jnp.sum(terms.astype(jnp.float32), axis=0))
    hidden = grid_states
    for iteration in range(ITERS):
        mixed = jnp.dot(hidden.reshape(-1, H), mix_weight, preferred_element_type=jnp.float32)
        mixed = mixed.astype(jnp.bfloat16).reshape(N_COL, N_ROW, BLK, H)
        coupled = lax.map(couple_group, (mixed, blocks_t, rows_t, cols_t, counts_t))
        hidden = normalize(hidden, coupled, gain, bias)
    restored = hidden.reshape(N_COL, N_ROW, N_COL, slice_rows, H)
    restored = jnp.transpose(restored, (1, 2, 0, 3, 4)).reshape(-1, H)
    return restored
```

```python
import functools

import jax
import jax.numpy as jnp
from jax import lax
from jax.experimental import pallas as pl
from jax.experimental.pallas import tpu as pltpu
from jax.sharding import PartitionSpec as P

ITERS = 2
ROW_TILE = 16
MESH_IDS = pl.DeviceIdType.MESH


def normalize(hidden, coupled, gain, bias):
    summed_in = hidden.astype(jnp.float32) + coupled
    mean_value = jnp.mean(summed_in, axis=-1, keepdims=True)
    centered = summed_in - mean_value
    variance = jnp.mean(centered * centered, axis=-1, keepdims=True)
    return (centered * lax.rsqrt(variance + 1e-05) * gain + bias).astype(jnp.bfloat16)


def to_grid(values):
    return lax.all_to_all(values, "col", split_axis=0, concat_axis=0, tiled=True)


def seat_layout(blocks, row_ids, col_ids, live_count, row_groups, seats_per_row):
    slot_total = row_ids.shape[0]
    block_len = blocks.shape[1]
    slot_ids = jnp.arange(slot_total, dtype=jnp.int32)
    live_mask = slot_ids < live_count
    earlier = (
        (row_ids[:, None] == row_ids[None, :])
        & (slot_ids[None, :] < slot_ids[:, None])
        & live_mask[None, :]
    )
    rank_in_row = jnp.sum(earlier.astype(jnp.int32), axis=1)
    seat_total = row_groups * seats_per_row
    seat_index = jnp.where(live_mask, row_ids * seats_per_row + rank_in_row, seat_total)
    seat_blocks = (
        jnp.zeros((seat_total, block_len, block_len), blocks.dtype)
        .at[seat_index]
        .set(blocks, mode="drop")
    )
    seat_cols = jnp.zeros((seat_total,), jnp.int32).at[seat_index].set(col_ids, mode="drop")
    return (
        seat_blocks.reshape(row_groups, seats_per_row, block_len, block_len),
        seat_cols.reshape(row_groups, seats_per_row),
    )


def couple(grid_mixed, prepared):
    gathered = lax.all_gather(grid_mixed, "row", axis=0, tiled=True)
    row_groups = lax.axis_size("row")
    block_len, feat_width = grid_mixed.shape
    pieces_all = gathered.reshape(row_groups, block_len, feat_width)
    seat_blocks, seat_cols = prepared
    chosen = (seat_cols[:, :, None] == jnp.arange(row_groups)).astype(grid_mixed.dtype)
    pieces = jnp.einsum(
        "skj,jbh->skbh", chosen, pieces_all, preferred_element_type=jnp.float32
    ).astype(grid_mixed.dtype)
    flat_sum = jnp.einsum(
        "skab,skbh->sah", seat_blocks, pieces, preferred_element_type=jnp.float32
    ).reshape(row_groups * block_len, feat_width)
    return lax.psum_scatter(
        flat_sum.astype(jnp.bfloat16), "row", scatter_dimension=0, tiled=True
    ).astype(jnp.float32)


def general_body(states, mix_weight, coherence, block_row, block_col, block_count, gain, bias):
    row_ids = block_row[0, 0]
    row_groups = lax.axis_size("row")
    slot_total = row_ids.shape[0]
    seats_per_row = max(2, (slot_total + row_groups - 1) // row_groups)
    prepared = seat_layout(
        coherence[0, 0], row_ids, block_col[0, 0], block_count[0, 0], row_groups, seats_per_row
    )
    hidden = to_grid(states)
    for iteration in range(ITERS):
        mixed = jnp.dot(hidden, mix_weight, preferred_element_type=jnp.float32).astype(jnp.bfloat16)
        hidden = normalize(hidden, couple(mixed, prepared), gain, bias)
    return to_grid(hidden)


def lowest_bit_index(bit):
    index = jnp.int32(0)
    for power, pattern in enumerate((-1431655766, -858993460, -252645136, -16711936, -65536)):
        index = index + jnp.where((bit & jnp.int32(pattern)) != 0, jnp.int32(1 << power), jnp.int32(0))
    return index


def link_kernel(
    n_col,
    seats,
    states,
    mix_weight,
    coherence,
    row_ids_in,
    col_ids_in,
    live_count_in,
    gain_in,
    bias_in,
    out,
    row_ids,
    col_ids,
    live_count,
    gain_row,
    bias_row,
    coh,
    weight,
    hall,
    hall2,
    fin,
    near_out,
    near_in,
    far_part,
    far_out,
    far_in,
    mate_out,
    mate_in,
    own_part,
    joint,
    load_sem,
    a2a_send,
    a2a_recv,
    blk_send,
    blk_recv,
    xc_send,
    xc_recv,
    fw_send,
    fw_recv,
    mate_send,
    mate_recv,
    x2_send,
    x2_recv,
    m2_send,
    m2_recv,
    f2_send,
    f2_recv,
    back_send,
    back_recv,
):
    r = lax.axis_index("row")
    c = lax.axis_index("col")
    blk = hall.shape[0] // 4
    part = blk // n_col
    slots = coh.shape[0]
    mate = (r ^ 1, c)
    across = (r ^ 2, c)

    def remote(src, dst, send_sem, recv_sem, device):
        return pltpu.make_async_remote_copy(
            src_ref=src, dst_ref=dst, send_sem=send_sem, recv_sem=recv_sem,
            device_id=device, device_id_type=MESH_IDS,
        )

    def rows_at(index, size=part):
        return pl.ds(pl.multiple_of(index * size, size), size)

    barrier = pltpu.get_barrier_semaphore()
    for step in range(1, n_col):
        pl.semaphore_signal(
            barrier, inc=1, device_id=(r, lax.rem(c + step, n_col)), device_id_type=MESH_IDS
        )
    for peer in (mate, across):
        pl.semaphore_signal(barrier, inc=1, device_id=peer, device_id_type=MESH_IDS)
    loads = [
        pltpu.make_async_copy(source, held, load_sem.at[4 + place])
        for place, (source, held) in enumerate(
            (
                (row_ids_in, row_ids),
                (col_ids_in, col_ids),
                (live_count_in, live_count),
                (gain_in, gain_row),
                (bias_in, bias_row),
            )
        )
    ]
    for load in loads:
        load.start()
    load_coh = pltpu.make_async_copy(coherence, coh, load_sem.at[0])
    load_weight = pltpu.make_async_copy(mix_weight, weight, load_sem.at[1])
    load_own = pltpu.make_async_copy(states.at[rows_at(c)], hall.at[rows_at(c)], load_sem.at[2])
    load_coh.start()
    load_own.start()
    load_weight.start()

    pl.semaphore_wait(barrier, n_col + 1)

    to_col = []
    for step in range(1, n_col):
        there = lax.rem(c + step, n_col)
        copy = remote(
            states.at[rows_at(there)], hall.at[rows_at(c)],
            a2a_send.at[step], a2a_recv.at[step], (r, there),
        )
        copy.start()
        to_col.append(copy)

    def cross(step):
        source = lax.rem(c + n_col - step, n_col)
        here = hall.at[rows_at(source)]
        slot2 = hall.at[pl.ds(pl.multiple_of(2 * blk + source * part, part), part)]
        slot3 = hall.at[pl.ds(pl.multiple_of(3 * blk + source * part, part), part)]
        over = remote(here, slot2, xc_send.at[step], xc_recv.at[step], across)
        onward = remote(slot2, slot3, fw_send.at[step], fw_recv.at[step], mate)
        return over, onward

    load_own.wait()
    crossings = [cross(step) for step in range(n_col)]
    crossings[0][0].start()

    for load in loads:
        load.wait()
    gain = gain_row[...].reshape(1, -1)
    bias = bias_row[...].reshape(1, -1)
    live = live_count[0, 0]
    row_bits = [jnp.int32(0)] * 4
    for k in range(slots):
        named = row_ids[k]
        bit = jnp.where(k < live, jnp.int32(1 << k if k < 31 else -(1 << 31)), jnp.int32(0))
        for q in range(4):
            row_bits[q] = row_bits[q] | jnp.where(named == (r ^ q), bit, jnp.int32(0))
    load_coh.wait()

    def partial(q, write):
        target = r ^ q
        bits = row_bits[q]
        places, scales = [], []
        for n in range(seats):
            low = bits & (-bits)
            place = lowest_bit_index(low)
            named = jnp.where(low != 0, col_ids[place] ^ target, jnp.int32(-1))
            places.append(place)
            scales.append(
                [jnp.where(named == t, jnp.float32(1), jnp.float32(0)) for t in range(4)]
            )
            bits = bits & (bits - 1)
        size = 32

        def some_rows(i, carry):
            rows = rows_at(i, size)
            sums = [jnp.zeros((size, blk), jnp.float32)] * 4
            for n in range(seats):
                block = coh[places[n], rows, :].astype(jnp.float32)
                sums = [sums[t] + block * scales[n][t] for t in range(4)]
            for t in range(4):
                write(rows, t, sums[t])
            return carry

        lax.fori_loop(0, blk // size, some_rows, 0)

    def into(ref):
        def write(rows, t, values):
            ref[rows, t * blk : (t + 1) * blk] = values.astype(ref.dtype)

        return write

    partial(3, into(near_out))
    near = remote(near_out, near_in, blk_send.at[0], blk_recv.at[0], mate)
    near.start()
    partial(2, into(far_part))
    near.wait_recv()
    far_out[...] = (far_part[...] + near_in[...].astype(jnp.float32)).astype(far_out.dtype)
    far = remote(far_out, far_in, blk_send.at[1], blk_recv.at[1], across)
    far.start()
    partial(1, into(mate_out))
    mated = remote(mate_out, mate_in, blk_send.at[2], blk_recv.at[2], mate)
    mated.start()
    partial(0, into(own_part))

    for step in range(1, n_col):
        to_col[step - 1].wait_recv()
        crossings[step][0].start()
    own_block = remote(hall.at[pl.ds(0, blk)], hall.at[pl.ds(blk, blk)], mate_send, mate_recv, mate)
    own_block.start()
    for over, onward in crossings:
        over.wait_recv()
        onward.start()

    mated.wait_recv()
    far.wait_recv()
    joint[...] = (
        own_part[...]
        + mate_in[...].astype(jnp.float32)
        + far_in[...].astype(jnp.float32)
    ).astype(joint.dtype)
    load_weight.wait()
    own_block.wait_recv()

    def product(source, low, high):
        return jnp.dot(
            joint[:, low * blk : high * blk], source[low * blk : high * blk, :],
            preferred_element_type=jnp.float32,
        )

    def settle(spread, source):
        return source[0:blk, :], jnp.dot(
            spread.astype(jnp.bfloat16), weight[...], preferred_element_type=jnp.float32
        )

    spread = product(hall, 0, 2)
    for over, onward in crossings:
        onward.wait_recv()
    spread = spread + product(hall, 2, 4)
    base, coupled = settle(spread, hall)

    quarters = 4
    size = blk // quarters
    sent = []
    for q in range(quarters):
        low, high = q * size, (q + 1) * size
        hall2[low:high, :] = normalize(base[low:high], coupled[low:high], gain, bias)
        here = hall2.at[pl.ds(low, size)]
        slot2 = hall2.at[pl.ds(2 * blk + low, size)]
        slot3 = hall2.at[pl.ds(3 * blk + low, size)]
        over = remote(here, slot2, x2_send.at[q], x2_recv.at[q], across)
        over.start()
        beside = remote(
            here, hall2.at[pl.ds(blk + low, size)], m2_send.at[q], m2_recv.at[q], mate
        )
        beside.start()
        onward = remote(slot2, slot3, f2_send.at[q], f2_recv.at[q], mate)
        sent.append((over, beside, onward))
    for over, beside, onward in sent:
        beside.wait_recv()
    spread = product(hall2, 0, 2)
    for over, beside, onward in sent:
        over.wait_recv()
        onward.start()
    spread = spread + product(hall2, 2, 3)
    for over, beside, onward in sent:
        onward.wait_recv()
    spread = spread + product(hall2, 3, 4)
    base, coupled = settle(spread, hall2)
    fin[...] = normalize(base, coupled, gain, bias)

    keep = pltpu.make_async_copy(fin.at[rows_at(c)], out.at[rows_at(c)], load_sem.at[3])
    back = []
    for step in range(1, n_col):
        there = lax.rem(c + step, n_col)
        copy = remote(
            fin.at[rows_at(there)], out.at[rows_at(c)],
            back_send.at[step], back_recv.at[step], (r, there),
        )
        copy.start()
        back.append(copy)
    keep.start()

    for copy in to_col:
        copy.wait_send()
    for over, onward in crossings:
        over.wait_send()
        onward.wait_send()
    for copy in (near, far, mated, own_block):
        copy.wait_send()
    for copies in sent:
        for copy in copies:
            copy.wait_send()
    keep.wait()
    for copy in back:
        copy.wait_send()
        copy.wait_recv()


def kernel_body(states, mix_weight, coherence, block_row, block_col, block_count, gain, bias):
    n_col = lax.axis_size("col")
    row_groups = lax.axis_size("row")
    blk, feat = states.shape
    slots = coherence.shape[2]
    seats = max(2, (slots + row_groups - 1) // row_groups)
    any_space = pl.BlockSpec(memory_space=pl.ANY)
    bf16, f32 = jnp.bfloat16, jnp.float32
    dma = pltpu.SemaphoreType.DMA
    wide = (blk, row_groups * blk)
    return pl.pallas_call(
        functools.partial(link_kernel, n_col, seats),
        out_shape=jax.ShapeDtypeStruct((blk, feat), bf16),
        in_specs=[any_space] * 8,
        out_specs=OUT_SPACE,
        scratch_shapes=[
            pltpu.SMEM((slots,), jnp.int32),
            pltpu.SMEM((slots,), jnp.int32),
            pltpu.SMEM((1, 1), jnp.int32),
            pltpu.VMEM((feat,), f32),
            pltpu.VMEM((feat,), f32),
            pltpu.VMEM((slots, blk, blk), bf16),
            pltpu.VMEM((feat, feat), bf16),
            pltpu.VMEM((row_groups * blk, feat), bf16),
            pltpu.VMEM((row_groups * blk, feat), bf16),
            pltpu.VMEM((blk, feat), bf16),
            pltpu.VMEM(wide, bf16),
            pltpu.VMEM(wide, bf16),
            pltpu.VMEM(wide, f32),
            pltpu.VMEM(wide, bf16),
            pltpu.VMEM(wide, bf16),
            pltpu.VMEM(wide, bf16),
            pltpu.VMEM(wide, bf16),
            pltpu.VMEM(wide, f32),
            pltpu.VMEM(wide, bf16),
            dma((9,)),
            dma((n_col,)),
            dma((n_col,)),
            dma((3,)),
            dma((3,)),
            dma((n_col,)),
            dma((n_col,)),
            dma((n_col,)),
            dma((n_col,)),
            dma,
            dma,
        ]
        + [dma((4,))] * 6
        + [dma((n_col,))] * 2,
        compiler_params=pltpu.CompilerParams(
            collective_id=0, has_side_effects=True, vmem_limit_bytes=60 << 20
        ),
    )(
        states,
        mix_weight,
        coherence.reshape(coherence.shape[2:]),
        block_row.reshape(slots),
        block_col.reshape(slots),
        block_count,
        gain,
        bias,
    )


OUT_SPACE = pl.BlockSpec(memory_space=pltpu.VMEM)


def solution(mesh):
    placed = (
        P(("row", "col"), None),
        P(),
        P("row", "col", None, None, None),
        P("row", "col", None),
        P("row", "col", None),
        P("row", "col"),
        P(),
        P(),
    )
    n_row, n_col = mesh.shape["row"], mesh.shape["col"]

    def body(*args):
        blk = args[0].shape[0]
        slots = args[2].shape[2]
        in_tiles = blk % n_col == 0 and (blk // n_col) % ROW_TILE == 0
        if n_row == 4 and n_col > 1 and in_tiles and slots <= 32:
            return kernel_body(*args)
        return general_body(*args)

    return jax.shard_map(
        body, mesh=mesh, in_specs=placed, out_specs=P(("row", "col"), None), check_vma=False
    )
```

```python
import functools

import jax
import jax.numpy as jnp
from jax import lax
from jax.experimental import pallas as pl
from jax.experimental.pallas import tpu as pltpu
from jax.sharding import PartitionSpec as P

ITERS = 2
ROW_TILE = 16
MESH_IDS = pl.DeviceIdType.MESH


def normalize(hidden, coupled, gain, bias):
    summed_in = hidden.astype(jnp.float32) + coupled
    mean_value = jnp.mean(summed_in, axis=-1, keepdims=True)
    centered = summed_in - mean_value
    variance = jnp.mean(centered * centered, axis=-1, keepdims=True)
    return (centered * lax.rsqrt(variance + 1e-05) * gain + bias).astype(jnp.bfloat16)


def to_grid(values):
    return lax.all_to_all(values, "col", split_axis=0, concat_axis=0, tiled=True)


def seat_layout(blocks, row_ids, col_ids, live_count, row_groups, seats_per_row):
    slot_total = row_ids.shape[0]
    block_len = blocks.shape[1]
    slot_ids = jnp.arange(slot_total, dtype=jnp.int32)
    live_mask = slot_ids < live_count
    earlier = (
        (row_ids[:, None] == row_ids[None, :])
        & (slot_ids[None, :] < slot_ids[:, None])
        & live_mask[None, :]
    )
    rank_in_row = jnp.sum(earlier.astype(jnp.int32), axis=1)
    seat_total = row_groups * seats_per_row
    seat_index = jnp.where(live_mask, row_ids * seats_per_row + rank_in_row, seat_total)
    seat_blocks = (
        jnp.zeros((seat_total, block_len, block_len), blocks.dtype)
        .at[seat_index]
        .set(blocks, mode="drop")
    )
    seat_cols = jnp.zeros((seat_total,), jnp.int32).at[seat_index].set(col_ids, mode="drop")
    return (
        seat_blocks.reshape(row_groups, seats_per_row, block_len, block_len),
        seat_cols.reshape(row_groups, seats_per_row),
    )


def couple(grid_mixed, prepared):
    gathered = lax.all_gather(grid_mixed, "row", axis=0, tiled=True)
    row_groups = lax.axis_size("row")
    block_len, feat_width = grid_mixed.shape
    pieces_all = gathered.reshape(row_groups, block_len, feat_width)
    seat_blocks, seat_cols = prepared
    chosen = (seat_cols[:, :, None] == jnp.arange(row_groups)).astype(grid_mixed.dtype)
    pieces = jnp.einsum(
        "skj,jbh->skbh", chosen, pieces_all, preferred_element_type=jnp.float32
    ).astype(grid_mixed.dtype)
    flat_sum = jnp.einsum(
        "skab,skbh->sah", seat_blocks, pieces, preferred_element_type=jnp.float32
    ).reshape(row_groups * block_len, feat_width)
    return lax.psum_scatter(
        flat_sum.astype(jnp.bfloat16), "row", scatter_dimension=0, tiled=True
    ).astype(jnp.float32)


def general_body(states, mix_weight, coherence, block_row, block_col, block_count, gain, bias):
    row_ids = block_row[0, 0]
    row_groups = lax.axis_size("row")
    slot_total = row_ids.shape[0]
    seats_per_row = max(2, (slot_total + row_groups - 1) // row_groups)
    prepared = seat_layout(
        coherence[0, 0], row_ids, block_col[0, 0], block_count[0, 0], row_groups, seats_per_row
    )
    hidden = to_grid(states)
    for iteration in range(ITERS):
        mixed = jnp.dot(hidden, mix_weight, preferred_element_type=jnp.float32).astype(jnp.bfloat16)
        hidden = normalize(hidden, couple(mixed, prepared), gain, bias)
    return to_grid(hidden)


def lowest_bit_index(bit):
    index = jnp.int32(0)
    for power, pattern in enumerate((-1431655766, -858993460, -252645136, -16711936, -65536)):
        index = index + jnp.where((bit & jnp.int32(pattern)) != 0, jnp.int32(1 << power), jnp.int32(0))
    return index


ORDER = (0, 2, 1, 3)


def link_kernel(
    n_col,
    seats,
    states,
    mix_weight,
    coherence,
    row_ids_in,
    col_ids_in,
    live_count_in,
    gain_in,
    bias_in,
    out,
    row_ids,
    col_ids,
    live_count,
    gain_row,
    bias_row,
    coh,
    weight,
    hall,
    hall2,
    fin,
    near_out,
    near_in,
    chip_sum,
    far_out,
    far_in,
    joint,
    load_sem,
    scatter_send,
    scatter_recv,
    pair_send,
    pair_recv,
    near_send,
    near_recv,
    far_send,
    far_recv,
    next_send,
    next_recv,
    back_send,
    back_recv,
):
    r = lax.axis_index("row")
    c = lax.axis_index("col")
    blk = hall.shape[0] // 4
    part = blk // n_col
    slots = coh.shape[0]
    mate = (r ^ 1, c)
    across = (r ^ 2, c)
    steps = tuple(range(n_col - 1, 0, -1))

    def remote(src, dst, send_sem, recv_sem, device):
        return pltpu.make_async_remote_copy(
            src_ref=src, dst_ref=dst, send_sem=send_sem, recv_sem=recv_sem,
            device_id=device, device_id_type=MESH_IDS,
        )

    def rows_at(index, size=part):
        return pl.ds(pl.multiple_of(index * size, size), size)

    barrier = pltpu.get_barrier_semaphore()
    for peer in (
        [(r ^ 2, c ^ step) for step in steps] + [(r, c ^ step) for step in steps] + [mate, across]
    ):
        pl.semaphore_signal(barrier, inc=1, device_id=peer, device_id_type=MESH_IDS)
    loads = [
        pltpu.make_async_copy(source, held, load_sem.at[4 + place])
        for place, (source, held) in enumerate(
            (
                (row_ids_in, row_ids),
                (col_ids_in, col_ids),
                (live_count_in, live_count),
                (gain_in, gain_row),
                (bias_in, bias_row),
            )
        )
    ]
    for load in loads[:3]:
        load.start()
    load_coh = pltpu.make_async_copy(coherence, coh, load_sem.at[0])
    load_weight = pltpu.make_async_copy(mix_weight, weight, load_sem.at[1])
    load_own = pltpu.make_async_copy(states.at[rows_at(c)], hall.at[rows_at(c)], load_sem.at[2])
    load_coh.start()
    load_own.start()
    load_weight.start()
    for load in loads[3:]:
        load.start()

    pl.semaphore_wait(barrier, 2 * n_col)

    over_rows = pl.ds(pl.multiple_of(blk + c * part, part), part)
    for step in steps + (0,):
        source = states.at[rows_at(c ^ step)]
        remote(
            source, hall.at[over_rows], scatter_send, scatter_recv.at[1], (r ^ 2, c ^ step)
        ).start()
        if step:
            remote(
                source, hall.at[rows_at(c)], scatter_send, scatter_recv.at[0], (r, c ^ step)
            ).start()

    def landed(low, size, send_sem, recv_sem):
        whole = hall.at[pl.ds(low, size)]
        return remote(whole, whole, send_sem, recv_sem, mate)

    for load in loads:
        load.wait()
    gain = gain_row[...].reshape(1, -1)
    bias = bias_row[...].reshape(1, -1)
    live = live_count[0, 0]
    row_bits = [jnp.int32(0)] * 4
    for k in range(slots):
        named = row_ids[k] ^ r
        bit = jnp.where(k < live, jnp.int32(1 << k if k < 31 else -(1 << 31)), jnp.int32(0))
        for q in range(4):
            row_bits[q] = row_bits[q] | jnp.where(named == q, bit, jnp.int32(0))
    load_coh.wait()

    def partial(q, reader, write):
        bits = row_bits[q]
        places, scales = [], []
        for n in range(seats):
            low = bits & (-bits)
            place = lowest_bit_index(low)
            named = jnp.where(low != 0, col_ids[place] ^ (r ^ reader), jnp.int32(-1))
            places.append(place)
            scales.append(
                [jnp.where(named == t, jnp.float32(1), jnp.float32(0)) for t in ORDER]
            )
            bits = bits & (bits - 1)
        size = 32

        def some_rows(i, carry):
            rows = rows_at(i, size)
            sums = [jnp.zeros((size, blk), jnp.float32)] * 4
            for n in range(seats):
                block = coh[places[n], rows, :].astype(jnp.float32)
                sums = [sums[t] + block * scales[n][t] for t in range(4)]
            for t in range(4):
                write(rows, t, sums[t])
            return carry

        lax.fori_loop(0, blk // size, some_rows, 0)

    def into(ref, half):
        def write(rows, t, values):
            ref[half, rows, t * blk : (t + 1) * blk] = values.astype(ref.dtype)

        return write

    near, far = [], []
    for half in range(2):
        partial((1, 3)[half], 1, into(near_out, half))
        near.append(
            remote(
                near_out.at[half], near_in.at[half],
                near_send.at[half], near_recv.at[half], mate,
            )
        )
        near[half].start()
    for half in range(2):
        partial((0, 2)[half], 0, into(chip_sum, half))
        near[half].wait_recv()
        chip_sum[half] = chip_sum[half] + near_in[half].astype(jnp.float32)
        far_out[half] = chip_sum[half].astype(far_out.dtype)
        far.append(
            remote(
                far_out.at[half], far_in.at[half], far_send.at[half], far_recv.at[half], across
            )
        )
        far[half].start()

    pairs = []
    load_own.wait()
    landed(0, blk - part, scatter_send, scatter_recv.at[0]).wait_recv()
    for half in range(2):
        if half:
            landed(0, blk, scatter_send, scatter_recv.at[1]).wait_recv()
        pairs.append(
            remote(
                hall.at[pl.ds(half * blk, blk)], hall.at[pl.ds((2 + half) * blk, blk)],
                pair_send.at[half], pair_recv.at[half], mate,
            )
        )
        pairs[half].start()
    load_weight.wait()

    for half in range(2):
        far[half].wait_recv()
        for t in range(4):
            mine = slice(t * blk, (t + 1) * blk)
            theirs = slice((t ^ 1) * blk, ((t ^ 1) + 1) * blk)
            joint[(1 - half) * blk : (2 - half) * blk, mine] = (
                chip_sum[1 - half, :, mine] + far_in[half, :, theirs].astype(jnp.float32)
            ).astype(joint.dtype)

    def product(rows, source, low, high):
        return jnp.dot(
            joint[rows, low * blk : high * blk], source[low * blk : high * blk, :],
            preferred_element_type=jnp.float32,
        )

    def settle(spread, rows, source):
        coupled = jnp.dot(
            spread.astype(jnp.bfloat16), weight[...], preferred_element_type=jnp.float32
        )
        return normalize(source[rows, :], coupled, gain, bias)

    halves = (slice(0, blk), slice(blk, 2 * blk))
    first = product(slice(0, 2 * blk), hall, 0, 2)
    for copy in pairs:
        copy.wait_recv()
    spread = first + product(slice(0, 2 * blk), hall, 2, 4)
    nexts = []
    for half, rows in enumerate(halves):
        hall2[rows, :] = settle(spread[rows], rows, hall)
        nexts.append(
            remote(
                hall2.at[pl.ds(half * blk, blk)], hall2.at[pl.ds((2 + half) * blk, blk)],
                next_send.at[half], next_recv.at[half], mate,
            )
        )
        nexts[half].start()
    first = product(halves[0], hall2, 0, 2)
    for copy in nexts:
        copy.wait_recv()
    fin[...] = settle(first + product(halves[0], hall2, 2, 4), halves[0], hall2)

    for step in steps:
        remote(
            fin.at[rows_at(c ^ step)], out.at[rows_at(c)], back_send, back_recv, (r, c ^ step)
        ).start()
    keep = pltpu.make_async_copy(fin.at[rows_at(c)], out.at[rows_at(c)], load_sem.at[3])
    keep.start()

    landed(0, 2 * blk - part, scatter_send, scatter_recv.at[0]).wait_send()
    for copy in near + far + pairs + nexts:
        copy.wait_send()
    keep.wait()
    returned = landed(0, blk - part, back_send, back_recv)
    returned.wait_recv()
    returned.wait_send()


def kernel_body(states, mix_weight, coherence, block_row, block_col, block_count, gain, bias):
    n_col = lax.axis_size("col")
    row_groups = lax.axis_size("row")
    blk, feat = states.shape
    slots = coherence.shape[2]
    seats = max(2, (slots + row_groups - 1) // row_groups)
    any_space = pl.BlockSpec(memory_space=pl.ANY)
    bf16, f32 = jnp.bfloat16, jnp.float32
    dma = pltpu.SemaphoreType.DMA
    wide = (2, blk, row_groups * blk)
    return pl.pallas_call(
        functools.partial(link_kernel, n_col, seats),
        out_shape=jax.ShapeDtypeStruct((blk, feat), bf16),
        in_specs=[any_space] * 8,
        out_specs=OUT_SPACE,
        scratch_shapes=[
            pltpu.SMEM((slots,), jnp.int32),
            pltpu.SMEM((slots,), jnp.int32),
            pltpu.SMEM((1, 1), jnp.int32),
            pltpu.VMEM((feat,), f32),
            pltpu.VMEM((feat,), f32),
            pltpu.VMEM((slots, blk, blk), bf16),
            pltpu.VMEM((feat, feat), bf16),
            pltpu.VMEM((row_groups * blk, feat), bf16),
            pltpu.VMEM((row_groups * blk, feat), bf16),
            pltpu.VMEM((blk, feat), bf16),
            pltpu.VMEM(wide, bf16),
            pltpu.VMEM(wide, bf16),
            pltpu.VMEM(wide, f32),
            pltpu.VMEM(wide, bf16),
            pltpu.VMEM(wide, bf16),
            pltpu.VMEM((2 * blk, row_groups * blk), bf16),
            dma((9,)),
            dma,
            dma((2,)),
        ]
        + [dma((2,))] * 8
        + [dma] * 2,
        compiler_params=pltpu.CompilerParams(
            collective_id=0, has_side_effects=True, vmem_limit_bytes=60 << 20
        ),
    )(
        states,
        mix_weight,
        coherence.reshape(coherence.shape[2:]),
        block_row.reshape(slots),
        block_col.reshape(slots),
        block_count,
        gain,
        bias,
    )


OUT_SPACE = pl.BlockSpec(memory_space=pltpu.VMEM)


def solution(mesh):
    placed = (
        P(("row", "col"), None),
        P(),
        P("row", "col", None, None, None),
        P("row", "col", None),
        P("row", "col", None),
        P("row", "col"),
        P(),
        P(),
    )
    n_row, n_col = mesh.shape["row"], mesh.shape["col"]

    def body(*args):
        blk = args[0].shape[0]
        slots = args[2].shape[2]
        in_tiles = blk % n_col == 0 and (blk // n_col) % ROW_TILE == 0
        pairs_up = n_col > 1 and n_col & (n_col - 1) == 0
        if n_row == 4 and pairs_up and in_tiles and slots <= 32:
            return kernel_body(*args)
        return general_body(*args)

    return jax.shard_map(
        body, mesh=mesh, in_specs=placed, out_specs=P(("row", "col"), None), check_vma=False
    )
```

```python
import functools

import jax
import jax.numpy as jnp
from jax import lax
from jax.experimental import pallas as pl
from jax.experimental.pallas import tpu as pltpu
from jax.sharding import PartitionSpec as P

ITERS = 2
ROW_TILE = 16
MESH_IDS = pl.DeviceIdType.MESH


def normalize(hidden, coupled, gain, bias):
    summed_in = hidden.astype(jnp.float32) + coupled
    mean_value = jnp.mean(summed_in, axis=-1, keepdims=True)
    centered = summed_in - mean_value
    variance = jnp.mean(centered * centered, axis=-1, keepdims=True)
    return (centered * lax.rsqrt(variance + 1e-05) * gain + bias).astype(jnp.bfloat16)


def to_grid(values):
    return lax.all_to_all(values, "col", split_axis=0, concat_axis=0, tiled=True)


def seat_layout(blocks, row_ids, col_ids, live_count, row_groups, seats_per_row):
    slot_total = row_ids.shape[0]
    block_len = blocks.shape[1]
    slot_ids = jnp.arange(slot_total, dtype=jnp.int32)
    live_mask = slot_ids < live_count
    earlier = (
        (row_ids[:, None] == row_ids[None, :])
        & (slot_ids[None, :] < slot_ids[:, None])
        & live_mask[None, :]
    )
    rank_in_row = jnp.sum(earlier.astype(jnp.int32), axis=1)
    seat_total = row_groups * seats_per_row
    seat_index = jnp.where(live_mask, row_ids * seats_per_row + rank_in_row, seat_total)
    seat_blocks = (
        jnp.zeros((seat_total, block_len, block_len), blocks.dtype)
        .at[seat_index]
        .set(blocks, mode="drop")
    )
    seat_cols = jnp.zeros((seat_total,), jnp.int32).at[seat_index].set(col_ids, mode="drop")
    return (
        seat_blocks.reshape(row_groups, seats_per_row, block_len, block_len),
        seat_cols.reshape(row_groups, seats_per_row),
    )


def couple(grid_mixed, prepared):
    gathered = lax.all_gather(grid_mixed, "row", axis=0, tiled=True)
    row_groups = lax.axis_size("row")
    block_len, feat_width = grid_mixed.shape
    pieces_all = gathered.reshape(row_groups, block_len, feat_width)
    seat_blocks, seat_cols = prepared
    chosen = (seat_cols[:, :, None] == jnp.arange(row_groups)).astype(grid_mixed.dtype)
    pieces = jnp.einsum(
        "skj,jbh->skbh", chosen, pieces_all, preferred_element_type=jnp.float32
    ).astype(grid_mixed.dtype)
    flat_sum = jnp.einsum(
        "skab,skbh->sah", seat_blocks, pieces, preferred_element_type=jnp.float32
    ).reshape(row_groups * block_len, feat_width)
    return lax.psum_scatter(
        flat_sum.astype(jnp.bfloat16), "row", scatter_dimension=0, tiled=True
    ).astype(jnp.float32)


def general_body(states, mix_weight, coherence, block_row, block_col, block_count, gain, bias):
    row_ids = block_row[0, 0]
    row_groups = lax.axis_size("row")
    slot_total = row_ids.shape[0]
    seats_per_row = max(2, (slot_total + row_groups - 1) // row_groups)
    prepared = seat_layout(
        coherence[0, 0], row_ids, block_col[0, 0], block_count[0, 0], row_groups, seats_per_row
    )
    hidden = to_grid(states)
    for iteration in range(ITERS):
        mixed = jnp.dot(hidden, mix_weight, preferred_element_type=jnp.float32).astype(jnp.bfloat16)
        hidden = normalize(hidden, couple(mixed, prepared), gain, bias)
    return to_grid(hidden)


def lowest_bit_index(bit):
    index = jnp.int32(0)
    for power, pattern in enumerate((-1431655766, -858993460, -252645136, -16711936, -65536)):
        index = index + jnp.where((bit & jnp.int32(pattern)) != 0, jnp.int32(1 << power), jnp.int32(0))
    return index


ORDER = (0, 2, 1, 3)


def link_kernel(
    n_col,
    seats,
    states,
    mix_weight,
    coherence,
    row_ids_in,
    col_ids_in,
    live_count_in,
    gain_in,
    bias_in,
    out,
    row_ids,
    col_ids,
    live_count,
    gain_row,
    bias_row,
    coh,
    weight,
    hall,
    hall2,
    fin,
    near_out,
    near_in,
    chip_sum,
    far_out,
    far_in,
    joint,
    load_sem,
    scatter_send,
    scatter_recv,
    pair_send,
    pair_recv,
    near_send,
    near_recv,
    far_send,
    far_recv,
    next_send,
    next_recv,
    back_send,
    back_recv,
):
    r = lax.axis_index("row")
    c = lax.axis_index("col")
    blk = hall.shape[0] // 4
    part = blk // n_col
    slots = coh.shape[0]
    mate = (r ^ 1, c)
    across = (r ^ 2, c)
    steps = tuple(range(n_col - 1, 0, -1))

    def remote(src, dst, send_sem, recv_sem, device):
        return pltpu.make_async_remote_copy(
            src_ref=src, dst_ref=dst, send_sem=send_sem, recv_sem=recv_sem,
            device_id=device, device_id_type=MESH_IDS,
        )

    def rows_at(index, size=part):
        return pl.ds(pl.multiple_of(index * size, size), size)

    barrier = pltpu.get_barrier_semaphore()
    for peer in (
        [(r ^ 2, c ^ step) for step in steps] + [(r, c ^ step) for step in steps] + [mate, across]
    ):
        pl.semaphore_signal(barrier, inc=1, device_id=peer, device_id_type=MESH_IDS)
    loads = [
        pltpu.make_async_copy(source, held, load_sem.at[4 + place])
        for place, (source, held) in enumerate(
            (
                (row_ids_in, row_ids),
                (col_ids_in, col_ids),
                (live_count_in, live_count),
                (gain_in, gain_row),
                (bias_in, bias_row),
            )
        )
    ]
    for load in loads[:3]:
        load.start()
    load_coh = pltpu.make_async_copy(coherence, coh, load_sem.at[0])
    load_weight = pltpu.make_async_copy(mix_weight, weight, load_sem.at[1])
    load_own = pltpu.make_async_copy(states.at[rows_at(c)], hall.at[rows_at(c)], load_sem.at[2])
    load_coh.start()
    load_own.start()
    load_weight.start()
    for load in loads[3:]:
        load.start()

    pl.semaphore_wait(barrier, 2 * n_col)

    over_rows = pl.ds(pl.multiple_of(blk + c * part, part), part)
    for step in steps + (0,):
        source = states.at[rows_at(c ^ step)]
        remote(
            source, hall.at[over_rows], scatter_send, scatter_recv.at[1], (r ^ 2, c ^ step)
        ).start()
        if step:
            remote(
                source, hall.at[rows_at(c)], scatter_send, scatter_recv.at[0], (r, c ^ step)
            ).start()

    def landed(low, size, send_sem, recv_sem):
        whole = hall.at[pl.ds(low, size)]
        return remote(whole, whole, send_sem, recv_sem, mate)

    for load in loads:
        load.wait()
    gain = gain_row[...].reshape(1, -1)
    bias = bias_row[...].reshape(1, -1)
    live = live_count[0, 0]
    row_bits = [jnp.int32(0)] * 4
    for k in range(slots):
        named = row_ids[k] ^ r
        bit = jnp.where(k < live, jnp.int32(1 << k if k < 31 else -(1 << 31)), jnp.int32(0))
        for q in range(4):
            row_bits[q] = row_bits[q] | jnp.where(named == q, bit, jnp.int32(0))
    load_coh.wait()

    def partial(q, reader, write):
        bits = row_bits[q]
        places, scales = [], []
        for n in range(seats):
            low = bits & (-bits)
            place = lowest_bit_index(low)
            named = jnp.where(low != 0, col_ids[place] ^ (r ^ reader), jnp.int32(-1))
            places.append(place)
            scales.append(
                [jnp.where(named == t, jnp.float32(1), jnp.float32(0)) for t in ORDER]
            )
            bits = bits & (bits - 1)
        size = 32

        def some_rows(i, carry):
            rows = rows_at(i, size)
            sums = [jnp.zeros((size, blk), jnp.float32)] * 4
            for n in range(seats):
                block = coh[places[n], rows, :].astype(jnp.float32)
                sums = [sums[t] + block * scales[n][t] for t in range(4)]
            for t in range(4):
                write(rows, t, sums[t])
            return carry

        lax.fori_loop(0, blk // size, some_rows, 0)

    def into(ref, half):
        def write(rows, t, values):
            ref[half, rows, t * blk : (t + 1) * blk] = values.astype(ref.dtype)

        return write

    near, far = [], []
    for half in range(2):
        partial((1, 3)[half], 1, into(near_out, half))
        near.append(
            remote(
                near_out.at[half], near_in.at[half],
                near_send.at[half], near_recv.at[half], mate,
            )
        )
        near[half].start()
        partial((0, 2)[half], 0, into(chip_sum, half))
        near[half].wait_recv()
        chip_sum[half] = chip_sum[half] + near_in[half].astype(jnp.float32)
        far_out[half] = chip_sum[half].astype(far_out.dtype)
        far.append(
            remote(
                far_out.at[half], far_in.at[half], far_send.at[half], far_recv.at[half], across
            )
        )
        far[half].start()

    pairs = []
    load_own.wait()
    landed(0, blk - part, scatter_send, scatter_recv.at[0]).wait_recv()
    for half in range(2):
        if half:
            landed(0, blk, scatter_send, scatter_recv.at[1]).wait_recv()
        pairs.append(
            remote(
                hall.at[pl.ds(half * blk, blk)], hall.at[pl.ds((2 + half) * blk, blk)],
                pair_send.at[half], pair_recv.at[half], mate,
            )
        )
        pairs[half].start()
    load_weight.wait()

    for half in range(2):
        far[half].wait_recv()
        for t in range(4):
            mine = slice(t * blk, (t + 1) * blk)
            theirs = slice((t ^ 1) * blk, ((t ^ 1) + 1) * blk)
            joint[(1 - half) * blk : (2 - half) * blk, mine] = (
                chip_sum[1 - half, :, mine] + far_in[half, :, theirs].astype(jnp.float32)
            ).astype(joint.dtype)

    def product(rows, source, low, high):
        return jnp.dot(
            joint[rows, low * blk : high * blk], source[low * blk : high * blk, :],
            preferred_element_type=jnp.float32,
        )

    def settle(spread, rows, source):
        coupled = jnp.dot(
            spread.astype(jnp.bfloat16), weight[...], preferred_element_type=jnp.float32
        )
        return normalize(source[rows, :], coupled, gain, bias)

    halves = (slice(0, blk), slice(blk, 2 * blk))
    first = product(slice(0, 2 * blk), hall, 0, 2)
    for copy in pairs:
        copy.wait_recv()
    spread = first + product(slice(0, 2 * blk), hall, 2, 4)
    nexts = []
    for half, rows in enumerate(halves):
        hall2[rows, :] = settle(spread[rows], rows, hall)
        nexts.append(
            remote(
                hall2.at[pl.ds(half * blk, blk)], hall2.at[pl.ds((2 + half) * blk, blk)],
                next_send.at[half], next_recv.at[half], mate,
            )
        )
        nexts[half].start()
    first = product(halves[0], hall2, 0, 2)
    for copy in nexts:
        copy.wait_recv()
    fin[...] = settle(first + product(halves[0], hall2, 2, 4), halves[0], hall2)

    for step in steps:
        remote(
            fin.at[rows_at(c ^ step)], out.at[rows_at(c)], back_send, back_recv, (r, c ^ step)
        ).start()
    keep = pltpu.make_async_copy(fin.at[rows_at(c)], out.at[rows_at(c)], load_sem.at[3])
    keep.start()

    landed(0, 2 * blk - part, scatter_send, scatter_recv.at[0]).wait_send()
    for copy in near + far + pairs + nexts:
        copy.wait_send()
    keep.wait()
    returned = landed(0, blk - part, back_send, back_recv)
    returned.wait_recv()
    returned.wait_send()


def kernel_body(states, mix_weight, coherence, block_row, block_col, block_count, gain, bias):
    n_col = lax.axis_size("col")
    row_groups = lax.axis_size("row")
    blk, feat = states.shape
    slots = coherence.shape[2]
    seats = max(2, (slots + row_groups - 1) // row_groups)
    any_space = pl.BlockSpec(memory_space=pl.ANY)
    bf16, f32 = jnp.bfloat16, jnp.float32
    dma = pltpu.SemaphoreType.DMA
    wide = (2, blk, row_groups * blk)
    return pl.pallas_call(
        functools.partial(link_kernel, n_col, seats),
        out_shape=jax.ShapeDtypeStruct((blk, feat), bf16),
        in_specs=[any_space] * 8,
        out_specs=OUT_SPACE,
        scratch_shapes=[
            pltpu.SMEM((slots,), jnp.int32),
            pltpu.SMEM((slots,), jnp.int32),
            pltpu.SMEM((1, 1), jnp.int32),
            pltpu.VMEM((feat,), f32),
            pltpu.VMEM((feat,), f32),
            pltpu.VMEM((slots, blk, blk), bf16),
            pltpu.VMEM((feat, feat), bf16),
            pltpu.VMEM((row_groups * blk, feat), bf16),
            pltpu.VMEM((row_groups * blk, feat), bf16),
            pltpu.VMEM((blk, feat), bf16),
            pltpu.VMEM(wide, bf16),
            pltpu.VMEM(wide, bf16),
            pltpu.VMEM(wide, f32),
            pltpu.VMEM(wide, bf16),
            pltpu.VMEM(wide, bf16),
            pltpu.VMEM((2 * blk, row_groups * blk), bf16),
            dma((9,)),
            dma,
            dma((2,)),
        ]
        + [dma((2,))] * 8
        + [dma] * 2,
        compiler_params=pltpu.CompilerParams(
            collective_id=0, has_side_effects=True, vmem_limit_bytes=60 << 20
        ),
    )(
        states,
        mix_weight,
        coherence.reshape(coherence.shape[2:]),
        block_row.reshape(slots),
        block_col.reshape(slots),
        block_count,
        gain,
        bias,
    )


OUT_SPACE = pl.BlockSpec(memory_space=pltpu.VMEM)


def solution(mesh):
    placed = (
        P(("row", "col"), None),
        P(),
        P("row", "col", None, None, None),
        P("row", "col", None),
        P("row", "col", None),
        P("row", "col"),
        P(),
        P(),
    )
    n_row, n_col = mesh.shape["row"], mesh.shape["col"]

    def body(*args):
        blk = args[0].shape[0]
        slots = args[2].shape[2]
        in_tiles = blk % n_col == 0 and (blk // n_col) % ROW_TILE == 0
        pairs_up = n_col > 1 and n_col & (n_col - 1) == 0
        if n_row == 4 and pairs_up and in_tiles and slots <= 32:
            return kernel_body(*args)
        return general_body(*args)

    return jax.shard_map(
        body, mesh=mesh, in_specs=placed, out_specs=P(("row", "col"), None), check_vma=False
    )
```
